128 devices in a mesh: ctx: 32 (over y, z, core), head: 4 (over x).
Axes of the slice: x: 4, y: 4, z: 4, core: 2. Of those that a mesh axis runs over, the one named last changes fastest.
Arguments:
- ctx_hidden: bfloat16 [32768, 4096], P('ctx', 'head')
- resp_hidden: bfloat16 [256, 4096], P('ctx', 'head')
- ctx_pos: int32 [32768], P('ctx'), may hold values from 0 to 65535, as said below
- resp_pos: int32 [256], P('ctx'), may hold values from 65536 to 66047, as said below
- input_norm_gain: float32 [4096], replicated, may hold values from 0.1 to 1.9
- q_weight: bfloat16 [4096, 4096], P(None, 'head'), may hold values from -127 to 127, as said below
- q_scale: float32 [4096], P('head'), as said below
- k_weight: bfloat16 [4096, 512], P(None, 'head'), may hold values from -127 to 127, as said below
- k_scale: float32 [512], P('head'), as said below
- v_weight: bfloat16 [4096, 512], P(None, 'head'), may hold values from -127 to 127, as said below
- v_scale: float32 [512], P('head'), as said below
Outputs:
- ctx_out: bfloat16 [32768, 4096], P('ctx', 'head')
- resp_out: bfloat16 [256, 4096], P('ctx', 'head')
The draws below stay inside these ranges and needn't reach their ends.
Inputs may be any that keep to these rules, and one draw needn't show every extreme that they name: `ctx_pos`: strictly increasing along the context, consecutive entries differ by 1 to 3. `resp_pos`: strictly increasing, continuing after the last context position, consecutive entries differ by 1 to 3. `q_weight`: whole numbers. `k_weight`: whole numbers. `v_weight`: whole numbers. `q_scale`: Positive. `k_scale`: Positive. `v_scale`: Positive.
All inputs are finite; a program needn't handle non-finite values.
Results may differ from the reference program's by a relative error of at most 0.017.
Values may be sent and summed in bfloat16 or wider, within the bound.
A program may use at most 192 MiB of HBM per device.

```python
import math
import jax
import jax.numpy as jnp
from jax import lax

D = 4096
HQ = 32
KVH = 4
HD = 128
BLK = 1024
RESP_DEV = 8
CTX = 32768
RESP = 256
N_CTX = 32


def column_scales(key):
    return jnp.exp(jax.random.uniform(jax.random.fold_in(key, 101), (D,), jnp.float32, 0.0, math.log(10.0)))


def hidden_rows(key, row_count, salt):
    columns = column_scales(key)
    key = jax.random.fold_in(key, salt)
    key_rows, key_values = jax.random.split(key, 2)
    scales = jnp.exp(jax.random.uniform(key_rows, (row_count, 1), jnp.float32, 0.0, math.log(10.0)))
    values = jax.random.truncated_normal(key_values, -6.0, 6.0, (row_count, D), jnp.float32)
    return (values * scales * columns[None, :]).astype(jnp.bfloat16)


def integer_codes(key, row_count, col_count):
    return jax.random.randint(key, (row_count, col_count), -127, 128, jnp.int32).astype(jnp.float32).astype(jnp.bfloat16)


def channel_scales(key, heads, base, head_spread):
    key_chan, key_head = jax.random.split(key)
    chan = jnp.exp(jax.random.uniform(key_chan, (heads, HD), jnp.float32, math.log(0.5), math.log(2.0)))
    per_head = jnp.exp(jax.random.uniform(key_head, (heads, 1), jnp.float32, 0.0, math.log(head_spread)))
    return (base * chan * per_head).reshape(heads * HD)


def all_positions(key):
    total_rows = CTX + RESP
    index = jnp.arange(total_rows, dtype=jnp.int32)
    jitter = jax.random.randint(jax.random.fold_in(key, 7), (total_rows,), 0, 2, jnp.int32)
    positions = 2 * index + jitter
    positions = jnp.where(index == 0, 0, positions)
    positions = jnp.where(index == CTX - 1, 2 * CTX - 1, positions)
    positions = jnp.where(index == CTX, 2 * CTX, positions)
    positions = jnp.where(index == total_rows - 1, 2 * total_rows - 1, positions)
    return positions


def draw_ctx_hidden(key, part):
    return hidden_rows(key, CTX, 11)


def draw_resp_hidden(key, part):
    return hidden_rows(key, RESP, 12)


def draw_ctx_pos(key, part):
    return all_positions(key)[:CTX]


def draw_resp_pos(key, part):
    return all_positions(key)[CTX:]


def draw_q_weight(key, part):
    key = jax.random.fold_in(key, 21)
    return integer_codes(key, D, HQ * HD)


def draw_k_weight(key, part):
    key = jax.random.fold_in(key, 22)
    return integer_codes(key, D, KVH * HD)


def draw_v_weight(key, part):
    key = jax.random.fold_in(key, 23)
    return integer_codes(key, D, KVH * HD)


def draw_q_scale(key, part):
    key = jax.random.fold_in(key, 31)
    spread = 1.0
    return channel_scales(key, HQ, 1.6 / (73.6 * math.sqrt(D)), spread)


def draw_k_scale(key, part):
    key = jax.random.fold_in(key, 32)
    spread = 1.0
    return channel_scales(key, KVH, 1.6 / (73.6 * math.sqrt(D)), spread)


def draw_v_scale(key, part):
    key = jax.random.fold_in(key, 33)
    spread = 1.0
    return channel_scales(key, KVH, 1.0 / (73.6 * math.sqrt(D)), spread)


def setup_inputs(seed: int = 0) -> dict:
    seeds = jax.random.split(jax.random.key(seed), 12)
    return {
        "ctx_hidden": draw_ctx_hidden(jax.random.fold_in(seeds[11], 71), 0),
        "resp_hidden": draw_resp_hidden(jax.random.fold_in(seeds[11], 71), 0),
        "ctx_pos": draw_ctx_pos(jax.random.fold_in(seeds[11], 71), 0),
        "resp_pos": draw_resp_pos(jax.random.fold_in(seeds[11], 71), 0),
        "input_norm_gain": jnp.clip(1.0 + 0.18 * jax.random.normal(seeds[4], (D,), jnp.float32), 0.1, 1.9),
        "q_weight": draw_q_weight(jax.random.fold_in(seeds[11], 71), 0),
        "q_scale": draw_q_scale(jax.random.fold_in(seeds[11], 71), 0),
        "k_weight": draw_k_weight(jax.random.fold_in(seeds[11], 71), 0),
        "k_scale": draw_k_scale(jax.random.fold_in(seeds[11], 71), 0),
        "v_weight": draw_v_weight(jax.random.fold_in(seeds[11], 71), 0),
        "v_scale": draw_v_scale(jax.random.fold_in(seeds[11], 71), 0),
    }


EPS = 1e-05
BASE = 500000.0
NEG = -1e+30

def rotate(vectors, positions):
    half_dim = vectors.shape[-1] // 2
    freqs = jnp.exp(jnp.arange(half_dim, dtype=jnp.float32) * (-2.0 * math.log(BASE) / vectors.shape[-1]))
    angles = positions.astype(jnp.float32)[:, None] * freqs[None, :]
    cosine = jnp.cos(angles)[:, None, :]
    sine = jnp.sin(angles)[:, None, :]
    front_part = vectors[..., :half_dim]
    second = vectors[..., half_dim:]
    return jnp.concatenate([front_part * cosine - second * sine, front_part * sine + second * cosine], axis=-1)

def apply_projection(input_rows, positions, input_norm_gain, q_weight, q_scale, k_weight, k_scale, v_weight, v_scale):
    values = input_rows.astype(jnp.float32)
    inverse = lax.rsqrt(lax.optimization_barrier(jnp.mean(values * values, axis=1)) + EPS)
    scaled = (values * input_norm_gain[None, :]).astype(jnp.bfloat16)
    scaled = lax.optimization_barrier(scaled).astype(jnp.float32)

    def project_one(matrix, column_scale):
        product = jnp.dot(scaled, matrix.astype(jnp.float32), precision=lax.Precision.HIGHEST)
        return product * column_scale[None, :] * inverse[:, None]
    row_total = input_rows.shape[0]
    query_rows = rotate(project_one(q_weight, q_scale).reshape(row_total, HQ, HD), positions).astype(jnp.bfloat16)
    key_rows = rotate(project_one(k_weight, k_scale).reshape(row_total, KVH, HD), positions).astype(jnp.bfloat16)
    value_rows = project_one(v_weight, v_scale).reshape(row_total, KVH, HD).astype(jnp.bfloat16)
    return (query_rows, key_rows, value_rows)

def as_float(weights):
    return lax.optimization_barrier(weights.astype(jnp.bfloat16)).astype(jnp.float32)

def reference(ctx_hidden, resp_hidden, ctx_pos, resp_pos, input_norm_gain, q_weight, q_scale, k_weight, k_scale, v_weight, v_scale):

    def encode(operands):
        block_hidden, block_pos = operands
        return apply_projection(block_hidden, block_pos, input_norm_gain, q_weight, q_scale, k_weight, k_scale, v_weight, v_scale)
    ctx_q, ctx_k, ctx_v = lax.map(encode, (ctx_hidden.reshape(N_CTX, BLK, D), ctx_pos.reshape(N_CTX, BLK)))
    resp_q, resp_k, resp_v = apply_projection(resp_hidden, resp_pos, input_norm_gain, q_weight, q_scale, k_weight, k_scale, v_weight, v_scale)
    groups = HQ // KVH
    ratio = 1.0 / math.sqrt(HD)
    anchor_keys = ctx_k[0].astype(jnp.float32)
    anchor_values = ctx_v[0].astype(jnp.float32)
    key_index = jnp.arange(2 * BLK, dtype=jnp.int32)
    query_index = jnp.arange(BLK, dtype=jnp.int32)

    def block_attention(operands):
        block_q, block_k, block_v, block_id = operands
        key_rows = jnp.concatenate([anchor_keys, block_k.astype(jnp.float32)], axis=0)
        value_rows = jnp.concatenate([anchor_values, block_v.astype(jnp.float32)], axis=0)
        query_rows = block_q.astype(jnp.float32).reshape(BLK, KVH, groups, HD)
        scores = jnp.einsum('nkgd,skd->kgns', query_rows, key_rows, precision=lax.Precision.HIGHEST) * ratio
        from_anchor = (key_index < BLK)[None, :] & (block_id > 0)
        from_own = (key_index >= BLK)[None, :] & ((key_index - BLK)[None, :] <= query_index[:, None])
        visible = from_anchor | from_own
        highest = lax.optimization_barrier(jnp.max(jnp.where(visible, scores, NEG), axis=-1, keepdims=True))
        weights = jnp.where(visible, jnp.exp(scores - highest), 0.0)
        denom = lax.optimization_barrier(jnp.sum(weights, axis=-1))
        mixed = jnp.einsum('kgns,skd->nkgd', as_float(weights), value_rows, precision=lax.Precision.HIGHEST)
        return (mixed / jnp.transpose(denom, (2, 0, 1))[..., None]).astype(jnp.bfloat16).reshape(BLK, HQ * HD)
    ctx_out = lax.map(block_attention, (ctx_q, ctx_k, ctx_v, jnp.arange(N_CTX, dtype=jnp.int32))).reshape(CTX, HQ * HD)
    resp_queries = resp_q.astype(jnp.float32).reshape(RESP, KVH, groups, HD)
    resp_keys = resp_k.reshape(N_CTX, RESP_DEV, KVH, HD)
    resp_values = resp_v.reshape(N_CTX, RESP_DEV, KVH, HD)
    all_index = jnp.arange(RESP, dtype=jnp.int32)

    def block_terms(block_k, block_v, extra_k, extra_v, block_id):
        scores_ctx = jnp.einsum('nkgd,skd->kgns', resp_queries, block_k.astype(jnp.float32), precision=lax.Precision.HIGHEST) * ratio
        scores_resp = jnp.einsum('nkgd,skd->kgns', resp_queries, extra_k.astype(jnp.float32), precision=lax.Precision.HIGHEST) * ratio
        extra_index = block_id * RESP_DEV + jnp.arange(RESP_DEV, dtype=jnp.int32)
        causal = extra_index[None, :] <= all_index[:, None]
        highest = jnp.maximum(lax.optimization_barrier(jnp.max(scores_ctx, axis=-1)), lax.optimization_barrier(jnp.max(jnp.where(causal, scores_resp, NEG), axis=-1)))
        weights_ctx = jnp.exp(scores_ctx - highest[..., None])
        weights_resp = jnp.where(causal, jnp.exp(scores_resp - highest[..., None]), 0.0)
        denom = lax.optimization_barrier(jnp.sum(weights_ctx, axis=-1)) + lax.optimization_barrier(jnp.sum(weights_resp, axis=-1))
        numer = jnp.einsum('kgns,skd->nkgd', as_float(weights_ctx), block_v.astype(jnp.float32), precision=lax.Precision.HIGHEST)
        numer = numer + jnp.einsum('kgns,skd->nkgd', as_float(weights_resp), extra_v.astype(jnp.float32), precision=lax.Precision.HIGHEST)
        return (jnp.transpose(highest, (2, 0, 1)), numer, jnp.transpose(denom, (2, 0, 1)))
    block_ids = jnp.arange(N_CTX, dtype=jnp.int32)

    def maxima_of(operands):
        block_k, block_v, extra_k, extra_v, block_id = operands
        return block_terms(block_k, block_v, extra_k, extra_v, block_id)[0]
    maxima = lax.map(maxima_of, (ctx_k, ctx_v, resp_keys, resp_values, block_ids))
    overall = lax.optimization_barrier(jnp.max(maxima, axis=0))

    def accumulate(carry, operands):
        block_k, block_v, extra_k, extra_v, block_id = operands
        highest, numer, denom = block_terms(block_k, block_v, extra_k, extra_v, block_id)
        factor = jnp.exp(highest - overall)
        return ((carry[0] + numer * factor[..., None], carry[1] + denom * factor), None)
    start_sums = (jnp.zeros((RESP, KVH, groups, HD), jnp.float32), jnp.zeros((RESP, KVH, groups), jnp.float32))
    totals, unused = lax.scan(accumulate, start_sums, (ctx_k, ctx_v, resp_keys, resp_values, block_ids))
    resp_out = (totals[0] / totals[1][..., None]).astype(jnp.bfloat16).reshape(RESP, HQ * HD)
    return (ctx_out, resp_out)
```

```python
import functools
import math

import jax
import jax.numpy as jnp
import numpy as np
from jax import lax
from jax.experimental import pallas as pl
from jax.experimental.pallas import tpu as pltpu
from jax.sharding import PartitionSpec as P

HD = 128
EPS = 1e-05
BASE = 500000.0
NEG = -1e30
RD = 8
MESH = pl.DeviceIdType.MESH
F32 = jnp.float32
BF16 = jnp.bfloat16
NX = 4


def nt(a, b):
    return lax.dot_general(a, b, (((1,), (1,)), ((), ())), preferred_element_type=F32)


def nn(a, b):
    return jnp.dot(a, b, preferred_element_type=F32)


def iota(shape, dim):
    return lax.broadcasted_iota(jnp.int32, shape, dim)


def kernel(
    n_ctx,
    chunks,
    hidden,
    resp_hidden,
    pos,
    resp_pos,
    gain,
    qw,
    kw,
    vw,
    q_scale,
    k_scale,
    v_scale,
    freq,
    ctx_out,
    resp_out,
    W,
    G,
    XS,
    SC,
    SCS,
    PF,
    PA,
    TC,
    TS,
    AG,
    KA,
    VA,
    RQ,
    K,
    V,
    KR,
    VR,
    Q,
    OUT,
    RM,
    RN,
    SB,
    RB,
    AUX,
    WT,
    lsem,
    scat_send,
    scat_recv,
    small_send,
    small_recv,
    ag_send,
    ag_recv,
    g_send,
    g_recv,
    r_send,
    r_recv,
    o_sem,
):
    blk, fs = hidden.shape
    full = NX * fs
    qc = q_scale.shape[1]
    heads = qc // HD
    ap = blk // n_ctx
    rr = heads * RD
    n_chunks = len(chunks)
    c = lax.axis_index("ctx")
    h = lax.axis_index("head")
    right = lax.rem(h + 1, NX)
    opp = lax.rem(h + 2, NX)
    left = lax.rem(h + 3, NX)

    loads = [
        pltpu.make_async_copy(qw, W.at[:, pl.ds(0, qc)], lsem.at[0]),
        pltpu.make_async_copy(kw, W.at[:, pl.ds(qc, HD)], lsem.at[1]),
        pltpu.make_async_copy(vw, W.at[:, pl.ds(qc + HD, HD)], lsem.at[2]),
        pltpu.make_async_copy(hidden, G.at[h], lsem.at[3]),
    ]

    barrier = pltpu.get_barrier_semaphore()

    def greet(d, carry):
        pl.semaphore_signal(
            barrier, inc=1, device_id=(lax.rem(c + d, n_ctx), h), device_id_type=MESH
        )
        return carry

    lax.fori_loop(1, n_ctx, greet, 0)
    for x in (left, right, opp):
        pl.semaphore_signal(barrier, inc=1, device_id=(c, x), device_id_type=MESH)
    PF[...] = pos[...].astype(F32)
    pl.semaphore_wait(barrier, n_ctx - 1 + 3)

    def remote(src, dst, ssem, rsem, dev):
        return pltpu.make_async_remote_copy(
            src_ref=src, dst_ref=dst, send_sem=ssem, recv_sem=rsem,
            device_id=dev, device_id_type=MESH,
        )

    def wait_bytes(ref, sem):
        pltpu.make_async_copy(ref, ref, sem).wait()

    def scat(d):
        return (
            remote(hidden.at[pl.ds(pl.multiple_of(d * ap, ap), ap)], XS.at[h, pl.ds(0, ap)],
                   scat_send.at[0], scat_recv.at[0], (d, h)),
            remote(PF, PA, scat_send.at[1], scat_recv.at[1], (d, h)),
        )

    own_piece = pltpu.make_async_copy(
        hidden.at[pl.ds(0, ap)], XS.at[h, pl.ds(0, ap)], lsem.at[4]
    )

    @pl.when(c == 0)
    def _():
        def go(d, carry):
            for copy in scat(d):
                copy.start()
            return carry

        lax.fori_loop(1, n_ctx, go, 0)
        own_piece.start()

    def own(j):
        r0, n = chunks[j]
        rows = pl.ds(r0, n)
        return (
            remote(hidden.at[rows], G.at[h, rows], g_send.at[j, 0], g_recv.at[j, 0], (c, right)),
            remote(hidden.at[rows], G.at[h, rows], g_send.at[j, 1], g_recv.at[j, 1], (c, left)),
        )

    def fwd(j):
        r0, n = chunks[j]
        a, b = pl.ds(r0, n // 2), pl.ds(r0 + n // 2, n // 2)
        return (
            remote(G.at[left, a], G.at[left, a], g_send.at[j, 2], g_recv.at[j, 2], (c, right)),
            remote(G.at[right, b], G.at[right, b], g_send.at[j, 3], g_recv.at[j, 3], (c, left)),
        )

    def start_own(j):
        if j < n_chunks:
            for copy in own(j):
                copy.start()

    def turn(j):
        if j < n_chunks:
            for copy in own(j):
                copy.wait_recv()
            for copy in fwd(j):
                copy.start()

    start_own(0)
    for copy in loads:
        copy.start()

    lane = iota((1, HD), 1)
    sign = jnp.where(lane < HD // 2, -1.0, 1.0).astype(F32)

    def tables(t, carry):
        column = jnp.transpose(jnp.broadcast_to(PF[pl.ds(t, 1), :], (HD, HD)))
        angle = column * freq[...]
        rows = pl.ds(pl.multiple_of(t * HD, HD), HD)
        TC[rows, :] = jnp.cos(angle)
        TS[rows, :] = jnp.sin(angle) * sign
        return carry

    lax.fori_loop(0, blk // HD, tables, 0)
    V[:, pl.ds(HD, HD)] = jnp.ones((blk, HD), BF16)
    VA[:, pl.ds(HD, HD)] = jnp.ones((blk, HD), BF16)
    KR[...] = jnp.zeros(KR.shape, BF16)
    VR[...] = jnp.zeros(VR.shape, BF16)
    WT[...] = jnp.zeros(WT.shape, F32)

    resp_rows = resp_hidden[...].astype(F32)
    XS[h, pl.ds(ap, 16), :] = jnp.concatenate([resp_rows, jnp.zeros_like(resp_rows)], 0).astype(BF16)

    @pl.when(c == 0)
    def _():
        PA[...] = PF[...]
        own_piece.wait()

    @pl.when(c > 0)
    def _():
        for copy in scat(0):
            copy.wait_recv()

    small = [
        remote(XS.at[h], XS.at[h], small_send.at[k], small_recv.at[k], (c, x))
        for k, x in enumerate((right, opp, left))
    ]
    for copy in small:
        copy.start()
    start_own(1)
    turn(0)
    start_own(2)

    def rotated(x, cosine, sine):
        return x * cosine + pltpu.roll(x, HD // 2, 1) * sine

    fold = math.log2(math.e) / math.sqrt(HD)

    anchor_pos = jnp.sum(
        jnp.where(
            iota((ap, HD), 1) == lax.rem(c * ap, HD) + iota((ap, HD), 0),
            jnp.broadcast_to(PA[pl.ds((c * ap) // HD, 1), :], (ap, HD)),
            0.0,
        ),
        axis=1, keepdims=True,
    )
    own_resp_pos = jnp.sum(
        jnp.where(
            iota((16, RD), 1) == iota((16, RD), 0),
            jnp.broadcast_to(resp_pos[...].astype(F32), (16, RD)),
            0.0,
        ),
        axis=1, keepdims=True,
    )
    angle = jnp.concatenate([anchor_pos, own_resp_pos], 0) * freq[...]
    small_cos = jnp.cos(angle)
    small_sin = jnp.sin(angle) * sign
    for copy in small:
        copy.wait_recv()
    for copy in loads:
        copy.wait()

    def scale_rows(src, rows, dst, n):
        squares = jnp.zeros((n, 1), F32)
        for s in range(NX):
            x = src[s, rows, :].astype(F32)
            squares += jnp.sum(x * x, axis=1, keepdims=True)
            dst[pl.ds(0, n), pl.ds(s * fs, fs)] = (x * gain[:, pl.ds(s * fs, fs)]).astype(BF16)
        return lax.rsqrt(squares / full + EPS)

    inverse = scale_rows(XS, pl.ds(0, ap + 16), SCS, ap + 16)
    small_cos = small_cos * inverse
    small_sin = small_sin * inverse
    kv = nn(SCS[...], W[:, pl.ds(qc, 2 * HD)])
    keys = rotated(kv[:, :HD] * k_scale[...], small_cos, small_sin)
    values = kv[:, HD:] * v_scale[...] * inverse
    AG[0, pl.ds(0, ap), :] = keys[:ap].astype(BF16)
    AG[0, pl.ds(ap, ap), :] = values[:ap].astype(BF16)
    KR[pl.ds(0, 16), :] = keys[ap:].astype(BF16)
    VR[pl.ds(0, 16), pl.ds(0, HD)] = values[ap:].astype(BF16)
    VR[pl.ds(0, 16), pl.ds(HD, HD)] = jnp.ones((16, HD), BF16)
    pieces = []
    for t in range(qc // (2 * HD)):
        cols = pl.ds(t * 2 * HD, 2 * HD)
        part = nn(SCS[pl.ds(ap, 16), :], W[:, cols]) * (q_scale[:, cols] * fold)
        for k in range(2):
            pieces.append(
                rotated(part[:, k * HD:(k + 1) * HD], small_cos[ap:], small_sin[ap:])[:RD]
            )
    AG[0, pl.ds(2 * ap, rr), :] = jnp.concatenate(pieces, 0).astype(BF16)

    def spread(d):
        return remote(AG.at[0], AG.at[d], ag_send.at[0], ag_recv.at[0],
                      (lax.rem(c + n_ctx - d, n_ctx), h))

    def send_spread(d, carry):
        spread(d).start()
        return carry

    lax.fori_loop(1, n_ctx, send_spread, 0)

    def project_kv(j, inverse, cosine, sine):
        r0, n = chunks[j]
        kv = nn(SC[pl.ds(0, n), :], W[:, pl.ds(qc, 2 * HD)])
        K[pl.ds(r0, n), :] = rotated(kv[:, :HD] * k_scale[...], cosine, sine).astype(BF16)
        V[pl.ds(r0, n), pl.ds(0, HD)] = (kv[:, HD:] * v_scale[...] * inverse).astype(BF16)

    def project_q(j, cosine, sine):
        r0, n = chunks[j]

        def step(t, carry):
            cols = pl.ds(pl.multiple_of(t * 2 * HD, 2 * HD), 2 * HD)
            part = nn(SC[pl.ds(0, n), :], W[:, cols]) * (q_scale[:, cols] * fold)
            for k in range(2):
                Q[2 * t + k, pl.ds(0, n), :] = rotated(
                    part[:, k * HD:(k + 1) * HD], cosine, sine
                ).astype(BF16)
            return carry

        lax.fori_loop(0, qc // (2 * HD), step, 0)

    def attend(j, with_anchor):
        r0, n = chunks[j]
        hs = max(1, min(heads, 256 // n))
        visible = iota((hs * n, n), 1) <= lax.rem(iota((hs * n, n), 0), n)

        def step(i, carry):
            q = Q[pl.ds(i * hs, hs), pl.ds(0, n), :].reshape(hs * n, HD)
            scores = [jnp.where(visible, nt(q, K[pl.ds(r0, n), :]), NEG)]
            vals = [V[pl.ds(r0, n), :]]
            if r0:
                scores.append(nt(q, K[pl.ds(0, r0), :]))
                vals.append(V[pl.ds(0, r0), :])
            if with_anchor:
                scores.append(nt(q, KA[...]))
                vals.append(VA[...])
            top = functools.reduce(
                jnp.maximum, [jnp.max(s, axis=1, keepdims=True) for s in scores]
            )
            total = None
            for s, v in zip(scores, vals):
                part = nn(jnp.exp2(s - top).astype(BF16), v)
                total = part if total is None else total + part
            mixed = (total[:, :HD] / total[:, HD:]).astype(BF16)
            for k in range(hs):
                OUT[pl.ds(r0, n), pl.ds(pl.multiple_of((i * hs + k) * HD, HD), HD)] = (
                    mixed[k * n:(k + 1) * n]
                )
            return carry

        lax.fori_loop(0, heads // hs, step, 0)

    def out_copy(j):
        r0, n = chunks[j]
        return pltpu.make_async_copy(
            OUT.at[pl.ds(r0, n)], ctx_out.at[pl.ds(r0, n)], o_sem.at[j]
        )

    ts = min(n_ctx, 256 // rr)
    tr = ts * rr
    last0, last_n = chunks[-1]

    def resp_first(i, carry):
        rows = pl.ds(pl.multiple_of(i * tr, tr), tr)
        q = RQ[rows, :]
        row = iota((tr, HD), 0)
        col = iota((tr, HD), 1)
        src = c + i * ts + row // rr
        src = jnp.where(src >= n_ctx, src - n_ctx, src)
        query = lax.rem(row, RD)
        seen = (col < RD) & (c * RD + col <= src * RD + query)
        s_own = jnp.where(seen, nt(q, KR[...]), NEG)
        s_ctx = nt(q, K[pl.ds(0, last0), :])
        top = jnp.maximum(
            jnp.max(s_own, axis=1, keepdims=True), jnp.max(s_ctx, axis=1, keepdims=True)
        )
        RN[rows, :] = nn(jnp.exp2(s_own - top).astype(BF16), VR[...]) + nn(
            jnp.exp2(s_ctx - top).astype(BF16), V[pl.ds(0, last0), :]
        )
        RM[rows, :] = jnp.broadcast_to(top, (tr, HD))
        return carry

    def give(d):
        return remote(SB.at[d], RB.at[n_ctx - 1 - d], r_send.at[0], r_recv.at[0],
                      (lax.rem(c + d, n_ctx), h))

    def resp_second(i, carry):
        rows = pl.ds(pl.multiple_of(i * tr, tr), tr)
        q = RQ[rows, :]
        s = nt(q, K[pl.ds(last0, last_n), :])
        before = RM[rows, :]
        top = jnp.maximum(before, jnp.max(s, axis=1, keepdims=True))
        factor = jnp.exp2(before - top)
        part = nn(jnp.exp2(s - top[:, :1]).astype(BF16), V[pl.ds(last0, last_n), :])
        num = RN[rows, pl.ds(0, HD)] * factor + part[:, :HD]
        den = RN[rows, pl.ds(HD, HD)] * factor + part[:, HD:]
        row = iota((rr, HD), 0)
        col = iota((rr, HD), 1)
        sub = iota((16, HD), 0)
        for k in range(ts):
            d = i * ts + k
            own_rows = slice(k * rr, (k + 1) * rr)
            SB[d, pl.ds(0, rr), :] = num[own_rows].astype(BF16)
            both = jnp.where(col == row, top[own_rows], 0.0) + jnp.where(
                col == row + 64, den[own_rows], 0.0
            )
            both = jnp.sum(both, axis=0, keepdims=True)
            high = both.astype(BF16).astype(F32)
            mid = (both - high).astype(BF16).astype(F32)
            low = both - high - mid
            SB[d, pl.ds(rr, 16), :] = jnp.where(
                sub == 0, high, jnp.where(sub == 1, mid, jnp.where(sub == 2, low, 0.0))
            ).astype(BF16)

            @pl.when(d > 0)
            def _():
                give(d).start()

        return carry

    def gathered():
        wait_bytes(AG.at[pl.ds(1, n_ctx - 1)], ag_recv.at[0])

        def place(d, carry):
            rows = pl.ds(pl.multiple_of(d * ap, ap), ap)
            KA[rows, :] = AG[d, pl.ds(0, ap), :]
            VA[rows, pl.ds(0, HD)] = AG[d, pl.ds(ap, ap), :]
            RQ[pl.ds(pl.multiple_of(d * rr, rr), rr), :] = AG[d, pl.ds(2 * ap, rr), :]
            return carry

        lax.fori_loop(0, n_ctx, place, 0)

    for j in range(n_chunks):
        r0, n = chunks[j]
        turn(j + 1)
        start_own(j + 3)
        for copy in fwd(j):
            copy.wait_recv()
        inverse = scale_rows(G, pl.ds(r0, n), SC, n)
        cosine = TC[pl.ds(r0, n), :] * inverse
        sine = TS[pl.ds(r0, n), :] * inverse
        project_kv(j, inverse, cosine, sine)
        if j == n_chunks - 1:
            lax.fori_loop(0, n_ctx // ts, resp_second, 0)
        project_q(j, cosine, sine)
        if j == 0:
            gathered()

        @pl.when(c > 0)
        def _():
            attend(j, True)

        @pl.when(c == 0)
        def _():
            attend(j, False)

        out_copy(j).start()
        if j == n_chunks - 2:
            lax.fori_loop(0, n_ctx // ts, resp_first, 0)

    wait_bytes(RB, r_recv.at[0])

    def unpack(k, carry):
        AUX[pl.ds(k, 1), :] = jnp.sum(RB[k, pl.ds(rr, 16), :].astype(F32), axis=0, keepdims=True)
        return carry

    lax.fori_loop(0, n_ctx - 1, unpack, 0)
    AUX[pl.ds(n_ctx - 1, 1), :] = jnp.sum(
        SB[0, pl.ds(rr, 16), :].astype(F32), axis=0, keepdims=True
    )
    both = AUX[...]
    weight = jnp.exp2(both - jnp.max(both, axis=0, keepdims=True))
    den = jnp.sum(weight * pltpu.roll(both, HD // 2, 1), axis=0, keepdims=True)
    WT[pl.ds(0, n_ctx), :] = jnp.where(iota((n_ctx, HD), 1) < rr, weight / den, 0.0)
    turned = jnp.transpose(WT[...])
    total = turned[:rr, n_ctx - 1:n_ctx] * SB[0, pl.ds(0, rr), :].astype(F32)
    for k in range(n_ctx - 1):
        total += turned[:rr, k:k + 1] * RB[k, pl.ds(0, rr), :].astype(F32)
    resp_out[...] = jnp.concatenate(
        [total[k * RD:(k + 1) * RD] for k in range(heads)], axis=1
    ).astype(BF16)

    for j in range(n_chunks):
        out_copy(j).wait()
        for copy in own(j) + fwd(j):
            copy.wait_send()
    for copy in small:
        copy.wait_send()
    wait_bytes(AG.at[pl.ds(1, n_ctx - 1)], ag_send.at[0])
    wait_bytes(SB.at[pl.ds(1, n_ctx - 1)], r_send.at[0])

    @pl.when(c == 0)
    def _():
        wait_bytes(hidden.at[pl.ds(0, (n_ctx - 1) * ap)], scat_send.at[0])
        wait_bytes(TC.at[pl.ds(0, (n_ctx - 1) * (blk // HD))], scat_send.at[1])


def local(
    ctx_hidden,
    resp_hidden,
    ctx_pos,
    resp_pos,
    input_norm_gain,
    q_weight,
    q_scale,
    k_weight,
    k_scale,
    v_weight,
    v_scale,
):
    n_ctx = lax.axis_size("ctx")
    blk, fs = ctx_hidden.shape
    full, qc = q_weight.shape
    heads = qc // HD
    ap = blk // n_ctx
    rr = heads * RD
    if blk >= 1024:
        sizes = (256, 256, 256, 128, 128)
    else:
        sizes = (blk // 2, blk // 4, blk // 4)
    starts = np.cumsum((0,) + sizes)
    chunks = [(int(a), int(n)) for a, n in zip(starts, sizes)]
    n_chunks = len(chunks)
    top = max(sizes)
    half = np.exp(np.arange(HD // 2, dtype=np.float64) * (-2.0 * math.log(BASE) / HD))
    freq = jnp.asarray(np.concatenate([half, half])[None, :].astype(np.float32))
    vm = pl.BlockSpec(memory_space=pltpu.VMEM)
    hbm = pl.BlockSpec(memory_space=pl.ANY)
    dma = pltpu.SemaphoreType.DMA
    scratch = [
        pltpu.VMEM((full, qc + 2 * HD), BF16),
        pltpu.VMEM((NX, blk, fs), BF16),
        pltpu.VMEM((NX, ap + 16, fs), BF16),
        pltpu.VMEM((top, full), BF16),
        pltpu.VMEM((ap + 16, full), BF16),
        pltpu.VMEM((blk // HD, HD), F32),
        pltpu.VMEM((blk // HD, HD), F32),
        pltpu.VMEM((blk, HD), F32),
        pltpu.VMEM((blk, HD), F32),
        pltpu.VMEM((n_ctx, 2 * ap + rr, HD), BF16),
        pltpu.VMEM((blk, HD), BF16),
        pltpu.VMEM((blk, 2 * HD), BF16),
        pltpu.VMEM((n_ctx * rr, HD), BF16),
        pltpu.VMEM((blk, HD), BF16),
        pltpu.VMEM((blk, 2 * HD), BF16),
        pltpu.VMEM((HD, HD), BF16),
        pltpu.VMEM((HD, 2 * HD), BF16),
        pltpu.VMEM((heads, top, HD), BF16),
        pltpu.VMEM((blk, qc), BF16),
        pltpu.VMEM((n_ctx * rr, HD), F32),
        pltpu.VMEM((n_ctx * rr, 2 * HD), F32),
        pltpu.VMEM((n_ctx, rr + 16, HD), BF16),
        pltpu.VMEM((n_ctx - 1, rr + 16, HD), BF16),
        pltpu.VMEM((n_ctx, HD), F32),
        pltpu.VMEM((HD, HD), F32),
        dma((5,)),
        dma((2,)),
        dma((2,)),
        dma((3,)),
        dma((3,)),
        dma((1,)),
        dma((1,)),
        dma((n_chunks, 4)),
        dma((n_chunks, 4)),
        dma((1,)),
        dma((1,)),
        dma((n_chunks,)),
    ]
    return pl.pallas_call(
        functools.partial(kernel, n_ctx, chunks),
        out_shape=(
            jax.ShapeDtypeStruct((blk, qc), BF16),
            jax.ShapeDtypeStruct((RD, qc), BF16),
        ),
        in_specs=[hbm, vm, vm, vm, vm, hbm, hbm, hbm, vm, vm, vm, vm],
        out_specs=(hbm, vm),
        scratch_shapes=scratch,
        compiler_params=pltpu.CompilerParams(
            collective_id=0, has_side_effects=True, vmem_limit_bytes=60 * 2**20
        ),
    )(
        ctx_hidden,
        resp_hidden,
        ctx_pos.reshape(blk // HD, HD),
        resp_pos.reshape(1, RD),
        input_norm_gain.reshape(1, full),
        q_weight,
        k_weight,
        v_weight,
        q_scale.reshape(1, qc),
        k_scale.reshape(1, HD),
        v_scale.reshape(1, HD),
        freq,
    )


def solution(mesh):
    return jax.shard_map(
        local,
        mesh=mesh,
        in_specs=(
            P("ctx", "head"),
            P("ctx", "head"),
            P("ctx"),
            P("ctx"),
            P(),
            P(None, "head"),
            P("head"),
            P(None, "head"),
            P("head"),
            P(None, "head"),
            P("head"),
        ),
        out_specs=(P("ctx", "head"), P("ctx", "head")),
        check_vma=False,
    )
```

```python
import functools
import math

import jax
import jax.numpy as jnp
import numpy as np
from jax import lax
from jax.experimental import pallas as pl
from jax.experimental.pallas import tpu as pltpu
from jax.sharding import PartitionSpec as P

HD = 128
EPS = 1e-05
BASE = 500000.0
NEG = -1e30
RD = 8
MESH = pl.DeviceIdType.MESH
F32 = jnp.float32
BF16 = jnp.bfloat16
NX = 4


def nt(a, b):
    return lax.dot_general(a, b, (((1,), (1,)), ((), ())), preferred_element_type=F32)


def nn(a, b):
    return jnp.dot(a, b, preferred_element_type=F32)


def iota(shape, dim):
    return lax.broadcasted_iota(jnp.int32, shape, dim)


def kernel(
    n_ctx,
    chunks,
    parcels,
    hidden,
    resp_hidden,
    pos,
    resp_pos,
    gain,
    qw,
    kw,
    vw,
    q_scale,
    k_scale,
    v_scale,
    freq,
    ctx_out,
    resp_out,
    W,
    G,
    XS,
    SC,
    SCS,
    PF,
    PA,
    TC,
    TS,
    AG,
    KA,
    VA,
    RQ,
    K,
    V,
    KR,
    VR,
    Q,
    OUT,
    RM,
    RN,
    SB,
    RB,
    AUX,
    WT,
    ST,
    MX,
    lsem,
    scat_send,
    scat_recv,
    small_send,
    small_recv,
    ag_send,
    ag_recv,
    g_send,
    g_recv,
    r_send,
    r_recv,
    o_sem,
):
    blk, fs = hidden.shape
    full = NX * fs
    qc = q_scale.shape[1]
    heads = qc // HD
    ap = blk // n_ctx
    rr = heads * RD
    n_chunks = len(chunks)
    n_parcels = len(parcels)
    c = lax.axis_index("ctx")
    h = lax.axis_index("head")
    right = lax.rem(h + 1, NX)
    opp = lax.rem(h + 2, NX)
    left = lax.rem(h + 3, NX)

    loads = [
        pltpu.make_async_copy(qw, W.at[:, pl.ds(0, qc)], lsem.at[0]),
        pltpu.make_async_copy(kw, W.at[:, pl.ds(qc, HD)], lsem.at[1]),
        pltpu.make_async_copy(vw, W.at[:, pl.ds(qc + HD, HD)], lsem.at[2]),
        pltpu.make_async_copy(hidden, G.at[h], lsem.at[3]),
    ]

    barrier = pltpu.get_barrier_semaphore()

    def greet(d, carry):
        pl.semaphore_signal(
            barrier, inc=1, device_id=(lax.rem(c + d, n_ctx), h), device_id_type=MESH
        )
        return carry

    lax.fori_loop(1, n_ctx, greet, 0)
    for x in (left, right, opp):
        pl.semaphore_signal(barrier, inc=1, device_id=(c, x), device_id_type=MESH)
    PF[...] = pos[...].astype(F32)
    pl.semaphore_wait(barrier, n_ctx - 1 + 3)

    def remote(src, dst, ssem, rsem, dev):
        return pltpu.make_async_remote_copy(
            src_ref=src, dst_ref=dst, send_sem=ssem, recv_sem=rsem,
            device_id=dev, device_id_type=MESH,
        )

    def wait_bytes(ref, sem):
        pltpu.make_async_copy(ref, ref, sem).wait()

    def scat(d):
        return (
            remote(hidden.at[pl.ds(pl.multiple_of(d * ap, ap), ap)], XS.at[h, pl.ds(0, ap)],
                   scat_send.at[0], scat_recv.at[0], (d, h)),
            remote(PF, PA, scat_send.at[1], scat_recv.at[1], (d, h)),
        )

    own_piece = pltpu.make_async_copy(
        hidden.at[pl.ds(0, ap)], XS.at[h, pl.ds(0, ap)], lsem.at[4]
    )

    @pl.when(c == 0)
    def _():
        def go(d, carry):
            for copy in scat(d):
                copy.start()
            return carry

        lax.fori_loop(1, n_ctx, go, 0)
        own_piece.start()

    def own(j):
        r0, n = parcels[j]
        rows = pl.ds(r0, n)
        return (
            remote(hidden.at[rows], G.at[h, rows], g_send.at[j, 0], g_recv.at[j, 0], (c, right)),
            remote(hidden.at[rows], G.at[h, rows], g_send.at[j, 1], g_recv.at[j, 1], (c, left)),
        )

    def fwd(j):
        r0, n = parcels[j]
        a, b = pl.ds(r0, n // 2), pl.ds(r0 + n // 2, n // 2)
        return (
            remote(G.at[left, a], G.at[left, a], g_send.at[j, 2], g_recv.at[j, 2], (c, right)),
            remote(G.at[right, b], G.at[right, b], g_send.at[j, 3], g_recv.at[j, 3], (c, left)),
        )

    def start_own(j):
        if j < n_parcels:
            for copy in own(j):
                copy.start()

    def turn(j):
        if j < n_parcels:
            for copy in own(j):
                copy.wait_recv()
            for copy in fwd(j):
                copy.start()

    def advance(j):
        turn(j)
        start_own(j + 2)

    start_own(0)
    start_own(1)
    for copy in loads:
        copy.start()

    lane = iota((1, HD), 1)
    sign = jnp.where(lane < HD // 2, -1.0, 1.0).astype(F32)

    def tables(t, carry):
        column = jnp.transpose(jnp.broadcast_to(PF[pl.ds(t, 1), :], (HD, HD)))
        angle = column * freq[...]
        rows = pl.ds(pl.multiple_of(t * HD, HD), HD)
        TC[rows, :] = jnp.cos(angle)
        TS[rows, :] = jnp.sin(angle) * sign
        return carry

    lax.fori_loop(0, blk // HD, tables, 0)
    V[:, pl.ds(HD, HD)] = jnp.ones((blk, HD), BF16)
    VA[:, pl.ds(HD, HD)] = jnp.ones((blk, HD), BF16)
    KR[...] = jnp.zeros(KR.shape, BF16)
    VR[...] = jnp.zeros(VR.shape, BF16)
    WT[...] = jnp.zeros(WT.shape, F32)

    resp_rows = resp_hidden[...].astype(F32)
    XS[h, pl.ds(ap, 16), :] = jnp.concatenate([resp_rows, jnp.zeros_like(resp_rows)], 0).astype(BF16)

    @pl.when(c == 0)
    def _():
        PA[...] = PF[...]
        own_piece.wait()

    @pl.when(c > 0)
    def _():
        for copy in scat(0):
            copy.wait_recv()

    small = [
        remote(XS.at[h], XS.at[h], small_send.at[k], small_recv.at[k], (c, x))
        for k, x in enumerate((right, opp, left))
    ]
    for copy in small:
        copy.start()
    advance(0)
    advance(1)

    def rotated(x, cosine, sine):
        return x * cosine + pltpu.roll(x, HD // 2, 1) * sine

    fold = math.log2(math.e) / math.sqrt(HD)

    anchor_pos = jnp.sum(
        jnp.where(
            iota((ap, HD), 1) == lax.rem(c * ap, HD) + iota((ap, HD), 0),
            jnp.broadcast_to(PA[pl.ds((c * ap) // HD, 1), :], (ap, HD)),
            0.0,
        ),
        axis=1, keepdims=True,
    )
    own_resp_pos = jnp.sum(
        jnp.where(
            iota((16, RD), 1) == iota((16, RD), 0),
            jnp.broadcast_to(resp_pos[...].astype(F32), (16, RD)),
            0.0,
        ),
        axis=1, keepdims=True,
    )
    angle = jnp.concatenate([anchor_pos, own_resp_pos], 0) * freq[...]
    small_cos = jnp.cos(angle)
    small_sin = jnp.sin(angle) * sign
    for copy in small:
        copy.wait_recv()
    for copy in loads:
        copy.wait()

    def scale_rows(src, rows, dst, n):
        squares = jnp.zeros((n, 1), F32)
        for s in range(NX):
            x = src[s, rows, :].astype(F32)
            squares += jnp.sum(x * x, axis=1, keepdims=True)
            dst[pl.ds(0, n), pl.ds(s * fs, fs)] = (x * gain[:, pl.ds(s * fs, fs)]).astype(BF16)
        return lax.rsqrt(squares / full + EPS)

    inverse = scale_rows(XS, pl.ds(0, ap + 16), SCS, ap + 16)
    small_cos = small_cos * inverse
    small_sin = small_sin * inverse
    kv = nn(SCS[...], W[:, pl.ds(qc, 2 * HD)])
    keys = rotated(kv[:, :HD] * k_scale[...], small_cos, small_sin)
    values = kv[:, HD:] * v_scale[...] * inverse
    AG[0, pl.ds(0, ap), :] = keys[:ap].astype(BF16)
    AG[0, pl.ds(ap, ap), :] = values[:ap].astype(BF16)
    KR[pl.ds(0, 16), :] = keys[ap:].astype(BF16)
    VR[pl.ds(0, 16), pl.ds(0, HD)] = values[ap:].astype(BF16)
    VR[pl.ds(0, 16), pl.ds(HD, HD)] = jnp.ones((16, HD), BF16)
    pieces = []
    for t in range(qc // (2 * HD)):
        cols = pl.ds(t * 2 * HD, 2 * HD)
        part = nn(SCS[pl.ds(ap, 16), :], W[:, cols]) * (q_scale[:, cols] * fold)
        for k in range(2):
            pieces.append(
                rotated(part[:, k * HD:(k + 1) * HD], small_cos[ap:], small_sin[ap:])[:RD]
            )
    AG[0, pl.ds(2 * ap, rr), :] = jnp.concatenate(pieces, 0).astype(BF16)

    def spread(d):
        return remote(AG.at[0], AG.at[d], ag_send.at[0], ag_recv.at[0],
                      (lax.rem(c + n_ctx - d, n_ctx), h))

    def send_spread(d, carry):
        spread(d).start()
        return carry

    lax.fori_loop(1, n_ctx, send_spread, 0)

    def project_kv(j, inverse, cosine, sine):
        r0, n = chunks[j]
        kv = nn(SC[pl.ds(0, n), :], W[:, pl.ds(qc, 2 * HD)])
        K[pl.ds(r0, n), :] = rotated(kv[:, :HD] * k_scale[...], cosine, sine).astype(BF16)
        V[pl.ds(r0, n), pl.ds(0, HD)] = (kv[:, HD:] * v_scale[...] * inverse).astype(BF16)

    def project_q(j, cosine, sine):
        r0, n = chunks[j]

        tiles = qc // (2 * HD)
        pair = 2 if tiles % 2 == 0 else 1

        def step(i, carry):
            for u in range(pair):
                t = i * pair + u
                cols = pl.ds(pl.multiple_of(t * 2 * HD, 2 * HD), 2 * HD)
                part = nn(SC[pl.ds(0, n), :], W[:, cols]) * (q_scale[:, cols] * fold)
                for k in range(2):
                    Q[2 * t + k, pl.ds(0, n), :] = rotated(
                        part[:, k * HD:(k + 1) * HD], cosine, sine
                    ).astype(BF16)
            return carry

        lax.fori_loop(0, tiles // pair, step, 0)

    def attend(j, with_anchor):
        r0, n = chunks[j]
        visible = iota((n, n), 1) <= iota((n, n), 0)
        spans = [(K, V, r0, n)]
        if r0:
            spans.append((K, V, 0, r0))
        if with_anchor:
            spans.append((KA, VA, 0, blk))

        def scores(i, slot):
            q = Q[i, pl.ds(0, n), :]
            top = None
            at = 0
            for k, (keys, _, start, size) in enumerate(spans):
                s = nt(q, keys[pl.ds(start, size), :])
                if k == 0:
                    s = jnp.where(visible, s, NEG)
                ST[slot, pl.ds(0, n), pl.ds(at, size)] = s
                at += size
                peak = jnp.max(s, axis=1, keepdims=True)
                top = peak if top is None else jnp.maximum(top, peak)
            MX[slot, pl.ds(0, n), :] = jnp.broadcast_to(top, (n, HD))

        def mix(i, slot):
            top = MX[slot, pl.ds(0, n), :][:, :1]
            total = None
            at = 0
            for _, vals, start, size in spans:
                p = jnp.exp2(ST[slot, pl.ds(0, n), pl.ds(at, size)] - top).astype(BF16)
                at += size
                part = nn(p, vals[pl.ds(start, size), :])
                total = part if total is None else total + part
            OUT[pl.ds(r0, n), pl.ds(pl.multiple_of(i * HD, HD), HD)] = (
                total[:, :HD] / total[:, HD:]
            ).astype(BF16)

        if not with_anchor:

            def plain(i, carry):
                scores(i, 0)
                mix(i, 0)
                return carry

            lax.fori_loop(0, heads, plain, 0)
            return

        scores(0, 0)

        def step(i, carry):
            mix(2 * i, 0)
            scores(2 * i + 1, 1)
            mix(2 * i + 1, 1)
            scores(lax.rem(2 * i + 2, heads), 0)
            return carry

        lax.fori_loop(0, heads // 2, step, 0)

    def out_copy(j):
        r0, n = chunks[j]
        return pltpu.make_async_copy(
            OUT.at[pl.ds(r0, n)], ctx_out.at[pl.ds(r0, n)], o_sem.at[j]
        )

    ts = min(n_ctx, 256 // rr)
    tr = ts * rr
    last0 = chunks[n_chunks // 2][0]
    last_n = blk - last0

    def resp_first(i, carry):
        rows = pl.ds(pl.multiple_of(i * tr, tr), tr)
        q = RQ[rows, :]
        row = iota((tr, HD), 0)
        col = iota((tr, HD), 1)
        src = c + i * ts + row // rr
        src = jnp.where(src >= n_ctx, src - n_ctx, src)
        query = lax.rem(row, RD)
        seen = (col < RD) & (c * RD + col <= src * RD + query)
        s_own = jnp.where(seen, nt(q, KR[...]), NEG)
        s_ctx = nt(q, K[pl.ds(0, last0), :])
        top = jnp.maximum(
            jnp.max(s_own, axis=1, keepdims=True), jnp.max(s_ctx, axis=1, keepdims=True)
        )
        RN[rows, :] = nn(jnp.exp2(s_own - top).astype(BF16), VR[...]) + nn(
            jnp.exp2(s_ctx - top).astype(BF16), V[pl.ds(0, last0), :]
        )
        RM[rows, :] = jnp.broadcast_to(top, (tr, HD))
        return carry

    def give(d):
        return remote(SB.at[d], RB.at[n_ctx - 1 - d], r_send.at[0], r_recv.at[0],
                      (lax.rem(c + d, n_ctx), h))

    def resp_second(i, carry):
        rows = pl.ds(pl.multiple_of(i * tr, tr), tr)
        q = RQ[rows, :]
        s = nt(q, K[pl.ds(last0, last_n), :])
        before = RM[rows, :]
        top = jnp.maximum(before, jnp.max(s, axis=1, keepdims=True))
        factor = jnp.exp2(before - top)
        part = nn(jnp.exp2(s - top[:, :1]).astype(BF16), V[pl.ds(last0, last_n), :])
        num = RN[rows, pl.ds(0, HD)] * factor + part[:, :HD]
        den = RN[rows, pl.ds(HD, HD)] * factor + part[:, HD:]
        row = iota((rr, HD), 0)
        col = iota((rr, HD), 1)
        sub = iota((16, HD), 0)
        for k in range(ts):
            d = i * ts + k
            own_rows = slice(k * rr, (k + 1) * rr)
            SB[d, pl.ds(0, rr), :] = num[own_rows].astype(BF16)
            both = jnp.where(col == row, top[own_rows], 0.0) + jnp.where(
                col == row + 64, den[own_rows], 0.0
            )
            both = jnp.sum(both, axis=0, keepdims=True)
            high = both.astype(BF16).astype(F32)
            mid = (both - high).astype(BF16).astype(F32)
            low = both - high - mid
            SB[d, pl.ds(rr, 16), :] = jnp.where(
                sub == 0, high, jnp.where(sub == 1, mid, jnp.where(sub == 2, low, 0.0))
            ).astype(BF16)

            @pl.when(d > 0)
            def _():
                give(d).start()

        return carry

    def by_pairs(work):
        tiles = n_ctx // ts
        pair = 2 if tiles % 2 == 0 else 1

        def step(i, carry):
            for u in range(pair):
                work(i * pair + u, 0)
            return carry

        lax.fori_loop(0, tiles // pair, step, 0)

    def gathered():
        wait_bytes(AG.at[pl.ds(1, n_ctx - 1)], ag_recv.at[0])

        def place(d, carry):
            rows = pl.ds(pl.multiple_of(d * ap, ap), ap)
            KA[rows, :] = AG[d, pl.ds(0, ap), :]
            VA[rows, pl.ds(0, HD)] = AG[d, pl.ds(ap, ap), :]
            RQ[pl.ds(pl.multiple_of(d * rr, rr), rr), :] = AG[d, pl.ds(2 * ap, rr), :]
            return carry

        lax.fori_loop(0, n_ctx, place, 0)

    for j in range(n_chunks):
        r0, n = chunks[j]
        advance(2 * j + 2)
        for copy in fwd(2 * j) + fwd(2 * j + 1):
            copy.wait_recv()
        inverse = scale_rows(G, pl.ds(r0, n), SC, n)
        cosine = TC[pl.ds(r0, n), :] * inverse
        sine = TS[pl.ds(r0, n), :] * inverse
        project_kv(j, inverse, cosine, sine)
        if j == n_chunks - 1:
            by_pairs(resp_second)
        project_q(j, cosine, sine)
        advance(2 * j + 3)
        if j == 0:
            gathered()

        @pl.when(c > 0)
        def _():
            attend(j, True)

        @pl.when(c == 0)
        def _():
            attend(j, False)

        out_copy(j).start()
        if j == n_chunks // 2 - 1:
            by_pairs(resp_first)

    wait_bytes(RB, r_recv.at[0])

    def unpack(k, carry):
        AUX[pl.ds(k, 1), :] = jnp.sum(RB[k, pl.ds(rr, 16), :].astype(F32), axis=0, keepdims=True)
        return carry

    lax.fori_loop(0, n_ctx - 1, unpack, 0)
    AUX[pl.ds(n_ctx - 1, 1), :] = jnp.sum(
        SB[0, pl.ds(rr, 16), :].astype(F32), axis=0, keepdims=True
    )
    both = AUX[...]
    weight = jnp.exp2(both - jnp.max(both, axis=0, keepdims=True))
    den = jnp.sum(weight * pltpu.roll(both, HD // 2, 1), axis=0, keepdims=True)
    WT[pl.ds(0, n_ctx), :] = jnp.where(iota((n_ctx, HD), 1) < rr, weight / den, 0.0)
    turned = jnp.transpose(WT[...])
    total = turned[:rr, n_ctx - 1:n_ctx] * SB[0, pl.ds(0, rr), :].astype(F32)
    for k in range(n_ctx - 1):
        total += turned[:rr, k:k + 1] * RB[k, pl.ds(0, rr), :].astype(F32)
    resp_out[...] = jnp.concatenate(
        [total[k * RD:(k + 1) * RD] for k in range(heads)], axis=1
    ).astype(BF16)

    for j in range(n_chunks):
        out_copy(j).wait()
    for j in range(n_parcels):
        for copy in own(j) + fwd(j):
            copy.wait_send()
    for copy in small:
        copy.wait_send()
    wait_bytes(AG.at[pl.ds(1, n_ctx - 1)], ag_send.at[0])
    wait_bytes(SB.at[pl.ds(1, n_ctx - 1)], r_send.at[0])

    @pl.when(c == 0)
    def _():
        wait_bytes(hidden.at[pl.ds(0, (n_ctx - 1) * ap)], scat_send.at[0])
        wait_bytes(TC.at[pl.ds(0, (n_ctx - 1) * (blk // HD))], scat_send.at[1])


def local(
    ctx_hidden,
    resp_hidden,
    ctx_pos,
    resp_pos,
    input_norm_gain,
    q_weight,
    q_scale,
    k_weight,
    k_scale,
    v_weight,
    v_scale,
):
    n_ctx = lax.axis_size("ctx")
    blk, fs = ctx_hidden.shape
    full, qc = q_weight.shape
    heads = qc // HD
    ap = blk // n_ctx
    rr = heads * RD
    n_chunks = 4 if blk >= 1024 else 2
    top = blk // n_chunks
    chunks = [(k * top, top) for k in range(n_chunks)]
    n_parcels = 2 * n_chunks
    parcels = [(k * (top // 2), top // 2) for k in range(n_parcels)]
    half = np.exp(np.arange(HD // 2, dtype=np.float64) * (-2.0 * math.log(BASE) / HD))
    freq = jnp.asarray(np.concatenate([half, half])[None, :].astype(np.float32))
    vm = pl.BlockSpec(memory_space=pltpu.VMEM)
    hbm = pl.BlockSpec(memory_space=pl.ANY)
    dma = pltpu.SemaphoreType.DMA
    scratch = [
        pltpu.VMEM((full, qc + 2 * HD), BF16),
        pltpu.VMEM((NX, blk, fs), BF16),
        pltpu.VMEM((NX, ap + 16, fs), BF16),
        pltpu.VMEM((top, full), BF16),
        pltpu.VMEM((ap + 16, full), BF16),
        pltpu.VMEM((blk // HD, HD), F32),
        pltpu.VMEM((blk // HD, HD), F32),
        pltpu.VMEM((blk, HD), F32),
        pltpu.VMEM((blk, HD), F32),
        pltpu.VMEM((n_ctx, 2 * ap + rr, HD), BF16),
        pltpu.VMEM((blk, HD), BF16),
        pltpu.VMEM((blk, 2 * HD), BF16),
        pltpu.VMEM((n_ctx * rr, HD), BF16),
        pltpu.VMEM((blk, HD), BF16),
        pltpu.VMEM((blk, 2 * HD), BF16),
        pltpu.VMEM((HD, HD), BF16),
        pltpu.VMEM((HD, 2 * HD), BF16),
        pltpu.VMEM((heads, top, HD), BF16),
        pltpu.VMEM((blk, qc), BF16),
        pltpu.VMEM((n_ctx * rr, HD), F32),
        pltpu.VMEM((n_ctx * rr, 2 * HD), F32),
        pltpu.VMEM((n_ctx, rr + 16, HD), BF16),
        pltpu.VMEM((n_ctx - 1, rr + 16, HD), BF16),
        pltpu.VMEM((n_ctx, HD), F32),
        pltpu.VMEM((HD, HD), F32),
        pltpu.VMEM((2, top, 2 * blk), F32),
        pltpu.VMEM((2, top, HD), F32),
        dma((5,)),
        dma((2,)),
        dma((2,)),
        dma((3,)),
        dma((3,)),
        dma((1,)),
        dma((1,)),
        dma((n_parcels, 4)),
        dma((n_parcels, 4)),
        dma((1,)),
        dma((1,)),
        dma((n_chunks,)),
    ]
    return pl.pallas_call(
        functools.partial(kernel, n_ctx, chunks, parcels),
        out_shape=(
            jax.ShapeDtypeStruct((blk, qc), BF16),
            jax.ShapeDtypeStruct((RD, qc), BF16),
        ),
        in_specs=[hbm, vm, vm, vm, vm, hbm, hbm, hbm, vm, vm, vm, vm],
        out_specs=(hbm, vm),
        scratch_shapes=scratch,
        compiler_params=pltpu.CompilerParams(
            collective_id=0, has_side_effects=True, vmem_limit_bytes=60 * 2**20
        ),
    )(
        ctx_hidden,
        resp_hidden,
        ctx_pos.reshape(blk // HD, HD),
        resp_pos.reshape(1, RD),
        input_norm_gain.reshape(1, full),
        q_weight,
        k_weight,
        v_weight,
        q_scale.reshape(1, qc),
        k_scale.reshape(1, HD),
        v_scale.reshape(1, HD),
        freq,
    )


def solution(mesh):
    return jax.shard_map(
        local,
        mesh=mesh,
        in_specs=(
            P("ctx", "head"),
            P("ctx", "head"),
            P("ctx"),
            P("ctx"),
            P(),
            P(None, "head"),
            P("head"),
            P(None, "head"),
            P("head"),
            P(None, "head"),
            P("head"),
        ),
        out_specs=(P("ctx", "head"), P("ctx", "head")),
        check_vma=False,
    )
```

```python
import functools
import math

import jax
import jax.numpy as jnp
import numpy as np
from jax import lax
from jax.experimental import pallas as pl
from jax.experimental.pallas import tpu as pltpu
from jax.sharding import PartitionSpec as P

HD = 128
EPS = 1e-05
BASE = 500000.0
NEG = -1e30
RD = 8
MESH = pl.DeviceIdType.MESH
F32 = jnp.float32
BF16 = jnp.bfloat16
NX = 4


def nt(a, b):
    return lax.dot_general(a, b, (((1,), (1,)), ((), ())), preferred_element_type=F32)


def nn(a, b):
    return jnp.dot(a, b, preferred_element_type=F32)


def iota(shape, dim):
    return lax.broadcasted_iota(jnp.int32, shape, dim)


def kernel(
    n_ctx,
    chunks,
    parcels,
    hidden,
    resp_hidden,
    pos,
    resp_pos,
    gain,
    qw,
    kw,
    vw,
    q_scale,
    k_scale,
    v_scale,
    freq,
    ctx_out,
    resp_out,
    W,
    G,
    XS,
    SC,
    SCS,
    PF,
    PA,
    TC,
    TS,
    AG,
    KA,
    VA,
    RQ,
    K,
    V,
    KR,
    VR,
    Q,
    OUT,
    RM,
    RN,
    SB,
    RB,
    WT,
    ST,
    MX,
    lsem,
    scat_send,
    scat_recv,
    small_send,
    small_recv,
    ag_send,
    ag_recv,
    g_send,
    g_recv,
    r_send,
    r_recv,
    o_sem,
):
    blk, fs = hidden.shape
    full = NX * fs
    qc = q_scale.shape[1]
    heads = qc // HD
    ap = blk // n_ctx
    rr = heads * RD
    n_chunks = len(chunks)
    n_parcels = len(parcels)
    c = lax.axis_index("ctx")
    h = lax.axis_index("head")
    right = lax.rem(h + 1, NX)
    opp = lax.rem(h + 2, NX)
    left = lax.rem(h + 3, NX)

    loads = [
        pltpu.make_async_copy(qw, W.at[:, pl.ds(0, qc)], lsem.at[0]),
        pltpu.make_async_copy(kw, W.at[:, pl.ds(qc, HD)], lsem.at[1]),
        pltpu.make_async_copy(vw, W.at[:, pl.ds(qc + HD, HD)], lsem.at[2]),
        pltpu.make_async_copy(hidden, G.at[h], lsem.at[3]),
    ]

    barrier = pltpu.get_barrier_semaphore()

    def greet(d, carry):
        pl.semaphore_signal(
            barrier, inc=1, device_id=(lax.rem(c + d, n_ctx), h), device_id_type=MESH
        )
        return carry

    lax.fori_loop(1, n_ctx, greet, 0)
    for x in (left, right, opp):
        pl.semaphore_signal(barrier, inc=1, device_id=(c, x), device_id_type=MESH)
    PF[...] = pos[...].astype(F32)
    pl.semaphore_wait(barrier, n_ctx - 1 + 3)

    def remote(src, dst, ssem, rsem, dev):
        return pltpu.make_async_remote_copy(
            src_ref=src, dst_ref=dst, send_sem=ssem, recv_sem=rsem,
            device_id=dev, device_id_type=MESH,
        )

    def wait_bytes(ref, sem):
        pltpu.make_async_copy(ref, ref, sem).wait()

    def scat(d):
        return (
            remote(hidden.at[pl.ds(pl.multiple_of(d * ap, ap), ap)], XS.at[h, pl.ds(0, ap)],
                   scat_send.at[0], scat_recv.at[0], (d, h)),
            remote(PF, PA, scat_send.at[1], scat_recv.at[1], (d, h)),
        )

    own_piece = pltpu.make_async_copy(
        hidden.at[pl.ds(0, ap)], XS.at[h, pl.ds(0, ap)], lsem.at[4]
    )

    @pl.when(c == 0)
    def _():
        def go(d, carry):
            for copy in scat(d):
                copy.start()
            return carry

        lax.fori_loop(1, n_ctx, go, 0)
        own_piece.start()

    def own(j):
        r0, n = parcels[j]
        rows = pl.ds(r0, n)
        return (
            remote(hidden.at[rows], G.at[h, rows], g_send.at[j, 0], g_recv.at[j, 0], (c, right)),
            remote(hidden.at[rows], G.at[h, rows], g_send.at[j, 1], g_recv.at[j, 1], (c, left)),
        )

    def fwd(j):
        r0, n = parcels[j]
        a, b = pl.ds(r0, n // 2), pl.ds(r0 + n // 2, n // 2)
        return (
            remote(G.at[left, a], G.at[left, a], g_send.at[j, 2], g_recv.at[j, 2], (c, right)),
            remote(G.at[right, b], G.at[right, b], g_send.at[j, 3], g_recv.at[j, 3], (c, left)),
        )

    def start_own(j):
        if j < n_parcels:
            for copy in own(j):
                copy.start()

    def turn(j):
        if j < n_parcels:
            for copy in own(j):
                copy.wait_recv()
            for copy in fwd(j):
                copy.start()

    def advance(j):
        turn(j)
        start_own(j + 2)

    start_own(0)
    start_own(1)
    for copy in loads:
        copy.start()

    lane = iota((1, HD), 1)
    sign = jnp.where(lane < HD // 2, -1.0, 1.0).astype(F32)

    def tables(t, carry):
        column = jnp.transpose(jnp.broadcast_to(PF[pl.ds(t, 1), :], (HD, HD)))
        angle = column * freq[...]
        rows = pl.ds(pl.multiple_of(t * HD, HD), HD)
        TC[rows, :] = jnp.cos(angle)
        TS[rows, :] = jnp.sin(angle) * sign
        return carry

    lax.fori_loop(0, blk // HD, tables, 0)
    V[:, pl.ds(HD, HD)] = jnp.ones((blk, HD), BF16)
    VA[:, pl.ds(HD, HD)] = jnp.ones((blk, HD), BF16)
    KR[...] = jnp.zeros(KR.shape, BF16)
    VR[...] = jnp.zeros(VR.shape, BF16)
    WT[...] = jnp.zeros(WT.shape, F32)

    def rotated(x, cosine, sine):
        return x * cosine + pltpu.roll(x, HD // 2, 1) * sine

    fold = math.log2(math.e) / math.sqrt(HD)

    def scale_rows(src, rows, dst, n, at=0):
        squares = jnp.zeros((n, 1), F32)
        for s in range(NX):
            x = src[s, rows, :].astype(F32)
            squares += jnp.sum(x * x, axis=1, keepdims=True)
            dst[pl.ds(at, n), pl.ds(s * fs, fs)] = (x * gain[:, pl.ds(s * fs, fs)]).astype(BF16)
        return lax.rsqrt(squares / full + EPS)

    def project_kv(r0, n, at):
        inverse = scale_rows(G, pl.ds(r0, n), SC, n, at)
        cosine = TC[pl.ds(r0, n), :] * inverse
        sine = TS[pl.ds(r0, n), :] * inverse
        TC[pl.ds(r0, n), :] = cosine
        TS[pl.ds(r0, n), :] = sine
        kv = nn(SC[pl.ds(at, n), :], W[:, pl.ds(qc, 2 * HD)])
        K[pl.ds(r0, n), :] = rotated(kv[:, :HD] * k_scale[...], cosine, sine).astype(BF16)
        V[pl.ds(r0, n), pl.ds(0, HD)] = (kv[:, HD:] * v_scale[...] * inverse).astype(BF16)

    def project_q(r0, n, at):
        part = nn(SC[pl.ds(at, n), :], W[:, pl.ds(0, qc)]) * (q_scale[...] * fold)
        cosine, sine = TC[pl.ds(r0, n), :], TS[pl.ds(r0, n), :]
        for k in range(heads):
            Q[k, pl.ds(at, n), :] = rotated(
                part[:, k * HD:(k + 1) * HD], cosine, sine
            ).astype(BF16)

    def arrived(p):
        for copy in fwd(p):
            copy.wait_recv()

    def early(p):
        arrived(p)
        project_kv(parcels[p][0], parcels[p][1], parcels[p][0])
        project_q(parcels[p][0], parcels[p][1], parcels[p][0])

    resp_rows = resp_hidden[...].astype(F32)
    XS[h, pl.ds(ap, 16), :] = jnp.concatenate([resp_rows, jnp.zeros_like(resp_rows)], 0).astype(BF16)

    turn(0)

    @pl.when(c == 0)
    def _():
        PA[...] = PF[...]
        own_piece.wait()

    @pl.when(c > 0)
    def _():
        for copy in scat(0):
            copy.wait_recv()

    small = [
        remote(XS.at[h], XS.at[h], small_send.at[k], small_recv.at[k], (c, x))
        for k, x in enumerate((right, opp, left))
    ]
    for copy in small:
        copy.start()
    start_own(2)
    advance(1)

    anchor_pos = jnp.sum(
        jnp.where(
            iota((ap, HD), 1) == lax.rem(c * ap, HD) + iota((ap, HD), 0),
            jnp.broadcast_to(PA[pl.ds((c * ap) // HD, 1), :], (ap, HD)),
            0.0,
        ),
        axis=1, keepdims=True,
    )
    own_resp_pos = jnp.sum(
        jnp.where(
            iota((16, RD), 1) == iota((16, RD), 0),
            jnp.broadcast_to(resp_pos[...].astype(F32), (16, RD)),
            0.0,
        ),
        axis=1, keepdims=True,
    )
    angle = jnp.concatenate([anchor_pos, own_resp_pos], 0) * freq[...]
    small_cos = jnp.cos(angle)
    small_sin = jnp.sin(angle) * sign
    for copy in loads:
        copy.wait()
    for copy in small:
        copy.wait_recv()

    inverse = scale_rows(XS, pl.ds(0, ap + 16), SCS, ap + 16)
    small_cos = small_cos * inverse
    small_sin = small_sin * inverse
    kv = nn(SCS[...], W[:, pl.ds(qc, 2 * HD)])
    keys = rotated(kv[:, :HD] * k_scale[...], small_cos, small_sin)
    values = kv[:, HD:] * v_scale[...] * inverse
    AG[0, pl.ds(0, ap), :] = keys[:ap].astype(BF16)
    AG[0, pl.ds(ap, ap), :] = values[:ap].astype(BF16)
    KR[pl.ds(0, 16), :] = keys[ap:].astype(BF16)
    VR[pl.ds(0, 16), pl.ds(0, HD)] = values[ap:].astype(BF16)
    VR[pl.ds(0, 16), pl.ds(HD, HD)] = jnp.ones((16, HD), BF16)
    pieces = []
    for t in range(qc // (2 * HD)):
        cols = pl.ds(t * 2 * HD, 2 * HD)
        part = nn(SCS[pl.ds(ap, 16), :], W[:, cols]) * (q_scale[:, cols] * fold)
        for k in range(2):
            pieces.append(
                rotated(part[:, k * HD:(k + 1) * HD], small_cos[ap:], small_sin[ap:])[:RD]
            )
    AG[0, pl.ds(2 * ap, rr), :] = jnp.concatenate(pieces, 0).astype(BF16)

    def spread(d):
        return remote(AG.at[0], AG.at[d], ag_send.at[0], ag_recv.at[0],
                      (lax.rem(c + n_ctx - d, n_ctx), h))

    def send_spread(d, carry):
        spread(d).start()
        return carry

    lax.fori_loop(1, n_ctx, send_spread, 0)
    early(0)
    advance(2)
    early(1)
    advance(3)

    def attend(j, with_anchor, lo, hi):
        r0, n = chunks[j]
        visible = iota((n, n), 1) <= iota((n, n), 0)
        spans = [(K, V, r0, n)]
        if r0:
            spans.append((K, V, 0, r0))
        if with_anchor:
            spans.append((KA, VA, 0, blk))

        def scores(i, slot):
            q = Q[i, pl.ds(0, n), :]
            top = None
            at = 0
            for k, (keys, _, start, size) in enumerate(spans):
                s = nt(q, keys[pl.ds(start, size), :])
                if k == 0:
                    s = jnp.where(visible, s, NEG)
                ST[slot, pl.ds(0, n), pl.ds(at, size)] = s
                at += size
                peak = jnp.max(s, axis=1, keepdims=True)
                top = peak if top is None else jnp.maximum(top, peak)
            MX[slot, pl.ds(0, n), :] = jnp.broadcast_to(top, (n, HD))

        def mix(i, slot):
            top = MX[slot, pl.ds(0, n), :][:, :1]
            total = None
            at = 0
            for _, vals, start, size in spans:
                p = jnp.exp2(ST[slot, pl.ds(0, n), pl.ds(at, size)] - top).astype(BF16)
                at += size
                part = nn(p, vals[pl.ds(start, size), :])
                total = part if total is None else total + part
            OUT[pl.ds(r0, n), pl.ds(pl.multiple_of(i * HD, HD), HD)] = (
                total[:, :HD] / total[:, HD:]
            ).astype(BF16)

        if not with_anchor:

            def plain(i, carry):
                scores(i, 0)
                mix(i, 0)
                return carry

            lax.fori_loop(lo, hi, plain, 0)
            return

        scores(lo, 0)

        def step(i, carry):
            mix(2 * i, 0)
            scores(2 * i + 1, 1)
            mix(2 * i + 1, 1)
            scores(lax.rem(2 * i + 2, heads), 0)
            return carry

        lax.fori_loop(lo // 2, hi // 2, step, 0)

    def out_copy(j):
        r0, n = chunks[j]
        return pltpu.make_async_copy(
            OUT.at[pl.ds(r0, n)], ctx_out.at[pl.ds(r0, n)], o_sem.at[j]
        )

    ts = min(n_ctx, 256 // rr)
    tr = ts * rr
    def resp_step(lo, hi, first):
        def work(i, carry):
            rows = pl.ds(pl.multiple_of(i * tr, tr), tr)
            q = RQ[rows, :]
            s_ctx = nt(q, K[pl.ds(lo, hi - lo), :])
            top = jnp.max(s_ctx, axis=1, keepdims=True)
            if first:
                row = iota((tr, HD), 0)
                col = iota((tr, HD), 1)
                src = c + i * ts + row // rr
                src = jnp.where(src >= n_ctx, src - n_ctx, src)
                query = lax.rem(row, RD)
                seen = (col < RD) & (c * RD + col <= src * RD + query)
                s_own = jnp.where(seen, nt(q, KR[...]), NEG)
                top = jnp.maximum(top, jnp.max(s_own, axis=1, keepdims=True))
                part = nn(jnp.exp2(s_own - top).astype(BF16), VR[...])
            else:
                before = RM[rows, :]
                top = jnp.maximum(before, top)
                factor = jnp.exp2(before - top)
                part = RN[rows, :] * jnp.concatenate([factor, factor], axis=1)
                top = top[:, :1]
            part += nn(jnp.exp2(s_ctx - top).astype(BF16), V[pl.ds(lo, hi - lo), :])
            return rows, top, part

        return work

    def resp_keep(lo, hi, first):
        def work(i, carry):
            rows, top, part = resp_step(lo, hi, first)(i, carry)
            RN[rows, :] = part
            RM[rows, :] = jnp.broadcast_to(top, (tr, HD))

        return work

    def give(d):
        return remote(SB.at[d], RB.at[n_ctx - 1 - d], r_send.at[0], r_recv.at[0],
                      (lax.rem(c + d, n_ctx), h))

    def resp_last(i, carry):
        _, top, part = resp_step(blk // 2, blk, False)(i, carry)
        top = jnp.broadcast_to(top, (tr, HD))
        num = part[:, :HD]
        den = part[:, HD:]
        row = iota((rr, HD), 0)
        col = iota((rr, HD), 1)
        sub = iota((16, HD), 0)
        for k in range(ts):
            d = i * ts + k
            own_rows = slice(k * rr, (k + 1) * rr)
            SB[d, pl.ds(0, rr), :] = num[own_rows].astype(BF16)
            both = jnp.where(col == row, top[own_rows], 0.0) + jnp.where(
                col == row + 64, den[own_rows], 0.0
            )
            both = jnp.sum(both, axis=0, keepdims=True)
            high = both.astype(BF16).astype(F32)
            mid = (both - high).astype(BF16).astype(F32)
            low = both - high - mid
            SB[d, pl.ds(rr, 16), :] = jnp.where(
                sub == 0, high, jnp.where(sub == 1, mid, jnp.where(sub == 2, low, 0.0))
            ).astype(BF16)

            @pl.when(d > 0)
            def _():
                give(d).start()

    def by_pairs(work):
        tiles = n_ctx // ts
        pair = 2 if tiles % 2 == 0 else 1

        def step(i, carry):
            for u in range(pair):
                work(i * pair + u, 0)
            return carry

        lax.fori_loop(0, tiles // pair, step, 0)

    def gathered():
        wait_bytes(AG.at[pl.ds(1, n_ctx - 1)], ag_recv.at[0])

        def place(d, carry):
            rows = pl.ds(pl.multiple_of(d * ap, ap), ap)
            KA[rows, :] = AG[d, pl.ds(0, ap), :]
            VA[rows, pl.ds(0, HD)] = AG[d, pl.ds(ap, ap), :]
            RQ[pl.ds(pl.multiple_of(d * rr, rr), rr), :] = AG[d, pl.ds(2 * ap, rr), :]
            return carry

        lax.fori_loop(0, n_ctx, place, 0)

    for j in range(n_chunks):
        r0, n = chunks[j]
        first, last = j == 0, j == n_chunks - 1
        if not first:
            advance(2 * j + 2)
        for p in (2 * j, 2 * j + 1) if last else ():
            arrived(p)
            project_kv(parcels[p][0], parcels[p][1], parcels[p][0] - r0)
        if last:
            by_pairs(resp_last)
        elif not first:
            arrived(2 * j)
            arrived(2 * j + 1)
            project_kv(r0, n, 0)
        if not first:
            project_q(r0, n, 0)
        else:
            gathered()

        middle = heads // 4 * 2 if not first and not last else 0
        for lo, hi in ((0, middle), (middle, heads)):
            if hi > lo:

                @pl.when(c > 0)
                def _():
                    attend(j, True, lo, hi)

                @pl.when(c == 0)
                def _():
                    attend(j, False, lo, hi)

            if lo == 0 and not first:
                advance(2 * j + 3)

        out_copy(j).start()
        if j == n_chunks // 2 - 1:
            by_pairs(resp_keep(0, r0 + n, True))

    for j in range(n_parcels):
        for copy in own(j) + fwd(j):
            copy.wait_send()
    for copy in small:
        copy.wait_send()
    wait_bytes(AG.at[pl.ds(1, n_ctx - 1)], ag_send.at[0])

    @pl.when(c == 0)
    def _():
        wait_bytes(hidden.at[pl.ds(0, (n_ctx - 1) * ap)], scat_send.at[0])
        wait_bytes(TC.at[pl.ds(0, (n_ctx - 1) * (blk // HD))], scat_send.at[1])

    wait_bytes(RB, r_recv.at[0])
    tail = pl.ds(rr, 16)
    both = jnp.concatenate(
        [
            jnp.sum(RB[:, tail, :].astype(F32), axis=1),
            jnp.sum(SB[0, tail, :].astype(F32), axis=0, keepdims=True),
        ],
        axis=0,
    )
    weight = jnp.exp2(both - jnp.max(both, axis=0, keepdims=True))
    den = jnp.sum(weight * pltpu.roll(both, HD // 2, 1), axis=0, keepdims=True)
    WT[pl.ds(0, n_ctx), :] = jnp.where(iota((n_ctx, HD), 1) < rr, weight / den, 0.0)
    turned = jnp.transpose(WT[...])
    total = turned[:rr, n_ctx - 1:n_ctx] * SB[0, pl.ds(0, rr), :].astype(F32)
    for k in range(n_ctx - 1):
        total += turned[:rr, k:k + 1] * RB[k, pl.ds(0, rr), :].astype(F32)
    resp_out[...] = jnp.concatenate(
        [total[k * RD:(k + 1) * RD] for k in range(heads)], axis=1
    ).astype(BF16)

    for j in range(n_chunks):
        out_copy(j).wait()
    wait_bytes(SB.at[pl.ds(1, n_ctx - 1)], r_send.at[0])


def local(
    ctx_hidden,
    resp_hidden,
    ctx_pos,
    resp_pos,
    input_norm_gain,
    q_weight,
    q_scale,
    k_weight,
    k_scale,
    v_weight,
    v_scale,
):
    n_ctx = lax.axis_size("ctx")
    blk, fs = ctx_hidden.shape
    full, qc = q_weight.shape
    heads = qc // HD
    ap = blk // n_ctx
    rr = heads * RD
    n_chunks = 4 if blk >= 1024 else 2
    top = blk // n_chunks
    chunks = [(k * top, top) for k in range(n_chunks)]
    n_parcels = 2 * n_chunks
    parcels = [(k * (top // 2), top // 2) for k in range(n_parcels)]
    half = np.exp(np.arange(HD // 2, dtype=np.float64) * (-2.0 * math.log(BASE) / HD))
    freq = jnp.asarray(np.concatenate([half, half])[None, :].astype(np.float32))
    vm = pl.BlockSpec(memory_space=pltpu.VMEM)
    hbm = pl.BlockSpec(memory_space=pl.ANY)
    dma = pltpu.SemaphoreType.DMA
    scratch = [
        pltpu.VMEM((full, qc + 2 * HD), BF16),
        pltpu.VMEM((NX, blk, fs), BF16),
        pltpu.VMEM((NX, ap + 16, fs), BF16),
        pltpu.VMEM((top, full), BF16),
        pltpu.VMEM((ap + 16, full), BF16),
        pltpu.VMEM((blk // HD, HD), F32),
        pltpu.VMEM((blk // HD, HD), F32),
        pltpu.VMEM((blk, HD), F32),
        pltpu.VMEM((blk, HD), F32),
        pltpu.VMEM((n_ctx, 2 * ap + rr, HD), BF16),
        pltpu.VMEM((blk, HD), BF16),
        pltpu.VMEM((blk, 2 * HD), BF16),
        pltpu.VMEM((n_ctx * rr, HD), BF16),
        pltpu.VMEM((blk, HD), BF16),
        pltpu.VMEM((blk, 2 * HD), BF16),
        pltpu.VMEM((HD, HD), BF16),
        pltpu.VMEM((HD, 2 * HD), BF16),
        pltpu.VMEM((heads, top, HD), BF16),
        pltpu.VMEM((blk, qc), BF16),
        pltpu.VMEM((n_ctx * rr, HD), F32),
        pltpu.VMEM((n_ctx * rr, 2 * HD), F32),
        pltpu.VMEM((n_ctx, rr + 16, HD), BF16),
        pltpu.VMEM((n_ctx - 1, rr + 16, HD), BF16),
        pltpu.VMEM((HD, HD), F32),
        pltpu.VMEM((2, top, 2 * blk), F32),
        pltpu.VMEM((2, top, HD), F32),
        dma((5,)),
        dma((2,)),
        dma((2,)),
        dma((3,)),
        dma((3,)),
        dma((1,)),
        dma((1,)),
        dma((n_parcels, 4)),
        dma((n_parcels, 4)),
        dma((1,)),
        dma((1,)),
        dma((n_chunks,)),
    ]
    return pl.pallas_call(
        functools.partial(kernel, n_ctx, chunks, parcels),
        out_shape=(
            jax.ShapeDtypeStruct((blk, qc), BF16),
            jax.ShapeDtypeStruct((RD, qc), BF16),
        ),
        in_specs=[hbm, vm, vm, vm, vm, hbm, hbm, hbm, vm, vm, vm, vm],
        out_specs=(hbm, vm),
        scratch_shapes=scratch,
        compiler_params=pltpu.CompilerParams(
            collective_id=0, has_side_effects=True, vmem_limit_bytes=60 * 2**20
        ),
    )(
        ctx_hidden,
        resp_hidden,
        ctx_pos.reshape(blk // HD, HD),
        resp_pos.reshape(1, RD),
        input_norm_gain.reshape(1, full),
        q_weight,
        k_weight,
        v_weight,
        q_scale.reshape(1, qc),
        k_scale.reshape(1, HD),
        v_scale.reshape(1, HD),
        freq,
    )


def solution(mesh):
    return jax.shard_map(
        local,
        mesh=mesh,
        in_specs=(
            P("ctx", "head"),
            P("ctx", "head"),
            P("ctx"),
            P("ctx"),
            P(),
            P(None, "head"),
            P("head"),
            P(None, "head"),
            P("head"),
            P(None, "head"),
            P("head"),
        ),
        out_specs=(P("ctx", "head"), P("ctx", "head")),
        check_vma=False,
    )
```
